32 devices in a mesh: grp: 2 (over y), ad: 4 (over z), tp: 4 (over x, core).
Axes of the slice: x: 2, y: 2, z: 4, core: 2. Of those that a mesh axis runs over, the one named last changes fastest.
Arguments:
- tokens: bfloat16 [512, 8192], P(('grp', 'ad'), 'tp'), parts along dimension 0, may hold values from -6 to 6
- row_adapter_index: int32 [512], P(('grp', 'ad')), parts along dimension 0, may hold values from 0 to 7, as said below
- adapter_slot_table: int32 [16], P('grp'), parts along dimension 0, may hold values from 0 to 7, as said below
- gate_matrix: bfloat16 [8192, 28672], P('tp', 'ad'), may hold values from -0.0625 to 0.0625
- down_weight_slots: bfloat16 [8, 64, 8192], P('ad', None, 'tp'), may hold values from -0.0625 to 0.0625
- up_weight_slots: bfloat16 [8, 64, 28672], P(None, 'tp', 'ad'), may hold values from -0.75 to 0.75
- slot_scale_table: float32 [8], replicated, may hold values from 0.3 to 3
Outputs:
- gated: bfloat16 [512, 28672], P(('grp', 'tp'), 'ad'), parts along dimension 0
The draws below stay inside these ranges and needn't reach their ends.
There are 2 independent parts, one for each index of `grp`. The reference program is written for one: setup_inputs(seed, part) draws one part's arguments, and reference() takes and returns one part's arrays. A program takes and returns all parts, laid end to end along the dimension named above; an argument that names none is the same for every part. Nothing has to cross between parts.
Inputs may be any that keep to these rules, and one draw needn't show every extreme that they name: A permutation: adapter a is stored at slot adapter_slot_table[a], and slot s belongs to index s // 2 of ad. `row_adapter_index`: at most 128 rows name adapters whose slots belong to one index of ad; in every draw one index has exactly 128.
All inputs are finite; a program needn't handle non-finite values.
Results may differ from the reference program's by a relative error of at most 0.015.
Values may be sent and summed in bfloat16 or wider, within the bound.
A program may use at most 128 MiB of HBM per device.

```python
import math
import jax
import jax.numpy as jnp
from jax import lax

MODEL_WIDTH = 8192
GATE_HIDDEN = 28672
ADAPTER_RANK = 64
AD_DEV = 2
ROWS = 256
ADAPTER_COUNT = 8
CAP = 128
N_AD = 4
N_TP = 4


def shared_routes(key):
    order = jax.random.permutation(jax.random.fold_in(key, 71), ADAPTER_COUNT).astype(jnp.int32)
    hottest = jax.random.randint(jax.random.fold_in(key, 72), (), 0, N_AD)
    index = jnp.arange(ROWS, dtype=jnp.int32)
    others = (hottest + 1 + (index - CAP) % (N_AD - 1)) % N_AD
    owner = jnp.where(index < CAP, hottest, others)
    owner = owner[jax.random.permutation(jax.random.fold_in(key, 73), ROWS)]
    local = jax.random.randint(jax.random.fold_in(key, 74), (ROWS,), 0, AD_DEV)
    slot = (owner * AD_DEV + local).astype(jnp.int32)
    inverse = jnp.zeros((ADAPTER_COUNT,), jnp.int32).at[order].set(jnp.arange(ADAPTER_COUNT, dtype=jnp.int32))
    return (order, inverse[slot])


def draw_adapter_slot_table(key, part):
    routes = shared_routes(key)
    return routes[0]


def draw_row_adapter_index(key, part):
    routes = shared_routes(key)
    return routes[1]


def block_levels(stream_key, extent, cuts, low, largest):
    def one(axis_at, parts):
        draws = jax.random.uniform(jax.random.fold_in(jax.random.fold_in(stream_key, 6), axis_at), (parts,), jnp.float32, low / len(cuts), largest / len(cuts))
        return jnp.repeat(jnp.exp(draws), extent[axis_at] // parts).reshape((-1,) + (1,) * (len(extent) - axis_at - 1))

    level = one(*cuts[0])
    for cut in cuts[1:]:
        level = level * one(*cut)
    return level


def centred(rng, dims, deviation, reach, cuts=(), kind=jnp.bfloat16):
    entries = jax.random.normal(rng, dims, jnp.float32) * deviation
    if len(cuts) > 0:
        entries = block_levels(rng, dims, cuts, -0.22, 0.18) * entries
    return jnp.clip(entries, min=-reach, max=reach).astype(kind)


def setup_inputs(seed: int = 0, part: int = 0) -> dict:
    seeds = jax.random.split(jax.random.key(seed), 8)
    part_keys = jax.random.split(jax.random.fold_in(seeds[7], part), 8)
    tokens = centred(part_keys[0], (ROWS, MODEL_WIDTH), 1.0, 6.0, ((0, 4), (1, 4)))
    row_adapter_index = draw_row_adapter_index(jax.random.fold_in(jax.random.fold_in(seeds[7], part), 71), part)
    adapter_slot_table = draw_adapter_slot_table(jax.random.fold_in(jax.random.fold_in(seeds[7], part), 71), part)
    gate_matrix = centred(seeds[3], (MODEL_WIDTH, GATE_HIDDEN), MODEL_WIDTH ** -0.5, 0.0625, ((0, 4), (1, 4)))
    down_weight_slots = centred(seeds[4], (ADAPTER_COUNT, ADAPTER_RANK, MODEL_WIDTH), MODEL_WIDTH ** -0.5, 0.0625, ((0, 4), (2, 4)))
    up_weight_slots = centred(seeds[5], (ADAPTER_COUNT, ADAPTER_RANK, GATE_HIDDEN), ADAPTER_RANK ** -0.5, 0.75, ((1, 4), (2, 4)))
    slot_scale_table = jnp.clip(jnp.exp(jax.random.uniform(seeds[6], (ADAPTER_COUNT,), jnp.float32, math.log(0.3), math.log(3.0))), 0.3, 3.0)
    return {"tokens": tokens, "row_adapter_index": row_adapter_index, "adapter_slot_table": adapter_slot_table, "gate_matrix": gate_matrix, "down_weight_slots": down_weight_slots, "up_weight_slots": up_weight_slots, "slot_scale_table": slot_scale_table}


def reference(tokens, row_adapter_index, adapter_slot_table, gate_matrix, down_weight_slots, up_weight_slots, slot_scale_table):
    slot_table = adapter_slot_table[row_adapter_index].astype(jnp.int32)
    row_scales = slot_scale_table[slot_table]
    block = math.gcd(ROWS, 64)
    count = ROWS // block
    slot_blocks = slot_table.reshape(count, block)

    def shrink_block(pair):
        rows_x, row_slot_index = pair
        down_matrices = down_weight_slots[row_slot_index].astype(jnp.float32)
        return jnp.einsum("rd,rkd->rk", rows_x.astype(jnp.float32), down_matrices)

    reduced_rank_output = lax.map(shrink_block, (tokens.reshape(count, block, MODEL_WIDTH), slot_blocks))
    reduced_rank_output = reduced_rank_output.reshape(ROWS, ADAPTER_RANK).astype(jnp.bfloat16)
    rank_portion = ADAPTER_RANK // N_TP
    feat_part = MODEL_WIDTH // N_TP
    total = jnp.zeros((ROWS, GATE_HIDDEN), jnp.float32)
    for adapter_group in range(N_TP):
        base = jnp.dot(tokens[:, adapter_group * feat_part:(adapter_group + 1) * feat_part],
                       gate_matrix[adapter_group * feat_part:(adapter_group + 1) * feat_part],
                       preferred_element_type=jnp.float32)
        up_matrices = up_weight_slots[:, adapter_group * rank_portion:(adapter_group + 1) * rank_portion]

        def expand_block(pair):
            rows_s, row_slot_index = pair
            down_matrices = up_matrices[row_slot_index].astype(jnp.float32)
            return jnp.einsum("rk,rkc->rc", rows_s.astype(jnp.float32), down_matrices)

        piece = reduced_rank_output[:, adapter_group * rank_portion:(adapter_group + 1) * rank_portion].reshape(count, block, rank_portion)
        delta = lax.map(expand_block, (piece, slot_blocks)).reshape(ROWS, GATE_HIDDEN)
        term = (base + row_scales[:, None] * delta).astype(jnp.bfloat16)
        term = lax.optimization_barrier(term)
        total = total + term.astype(jnp.float32)
    return total.astype(jnp.bfloat16)
```

```python
import functools

import jax
import jax.numpy as jnp
from jax import lax
from jax.experimental import pallas as pl
from jax.experimental.pallas import tpu as pltpu
from jax.sharding import PartitionSpec as P

PHASES = 2
CHUNKS = 7
EARLY = 3
MESH = pl.DeviceIdType.MESH
F32 = jnp.float32
BF16 = jnp.bfloat16


def kernel(
    n_ad,
    n_tp,
    tokens,
    ids,
    table,
    scales,
    gate,
    down,
    up,
    out,
    x_all,
    w,
    dn,
    upv,
    acc,
    meta_own,
    meta_in,
    slots,
    scale_cols,
    a_send,
    a_recv,
    b_send,
    b_recv,
    spread,
    expand,
    send1,
    recv1,
    keep,
    send2,
    recv2,
    w_sem,
    local_sem,
    x_ssem,
    x_rsem,
    m_ssem,
    m_rsem,
    a_ssem,
    a_rsem,
    b_ssem,
    b_rsem,
    s1_ssem,
    s1_rsem,
    s2_ssem,
    s2_rsem,
):
    me_ad = lax.axis_index("ad")
    me_tp = lax.axis_index("tp")
    core = lax.rem(me_tp, 2)
    me_x = me_tp // 2
    n_x = n_tp // 2
    rows_dev = tokens.shape[0]
    hp = rows_dev // PHASES
    rows = n_ad * hp
    cw = gate.shape[1] // CHUNKS
    tile = 256 if cw % 256 == 0 else cw
    rank_part = a_recv.shape[2]
    rank = rank_part * n_tp
    owned = down.shape[0] // rank
    n_slots = scales.shape[0]
    per_dest = rows // n_tp
    blocks = n_ad // n_tp

    def cols(j):
        return pl.ds(pl.multiple_of(j * cw, cw), cw)

    def ad_peer(k):
        return {"ad": lax.rem(me_ad + k, n_ad)}

    def tp_peer(k):
        return {"tp": lax.rem(me_tp + k, n_tp)}

    def w_copy(j):
        return pltpu.make_async_copy(gate.at[:, cols(j)], w.at[:, cols(j)], w_sem.at[j])

    dn_copy = pltpu.make_async_copy(down, dn, local_sem.at[0])
    up_copy = pltpu.make_async_copy(up, upv, local_sem.at[1])

    def own_rows(p):
        return x_all.at[p, pl.ds(pl.multiple_of(me_ad * hp, hp), hp)]

    def own_copy(p):
        return pltpu.make_async_copy(
            tokens.at[pl.ds(p * hp, hp)], own_rows(p), local_sem.at[2 + p]
        )

    def x_send(p, k):
        return pltpu.make_async_remote_copy(
            src_ref=tokens.at[pl.ds(p * hp, hp)],
            dst_ref=own_rows(p),
            send_sem=x_ssem.at[p, k - 1],
            recv_sem=x_rsem.at[p, k - 1],
            device_id=ad_peer(k),
            device_id_type=MESH,
        )

    def x_recv(p, k):
        origin = lax.rem(me_ad + n_ad - k, n_ad)
        return pltpu.make_async_remote_copy(
            src_ref=tokens.at[pl.ds(p * hp, hp)],
            dst_ref=x_all.at[p, pl.ds(pl.multiple_of(origin * hp, hp), hp)],
            send_sem=x_ssem.at[p, k - 1],
            recv_sem=x_rsem.at[p, k - 1],
            device_id=ad_peer(k),
            device_id_type=MESH,
        )

    def m_copy(k):
        return pltpu.make_async_remote_copy(
            src_ref=meta_own,
            dst_ref=meta_in.at[k - 1],
            send_sem=m_ssem.at[k - 1],
            recv_sem=m_rsem.at[k - 1],
            device_id=ad_peer(k),
            device_id_type=MESH,
        )

    def a_copy(p, k):
        return pltpu.make_async_remote_copy(
            src_ref=a_send.at[p, lax.rem(me_tp + k, n_tp)],
            dst_ref=a_recv.at[p, k - 1],
            send_sem=a_ssem.at[p, k - 1],
            recv_sem=a_rsem.at[p, k - 1],
            device_id=tp_peer(k),
            device_id_type=MESH,
        )

    def b_copy(p, k):
        return pltpu.make_async_remote_copy(
            src_ref=b_send.at[p],
            dst_ref=b_recv.at[p, k - 1],
            send_sem=b_ssem.at[p, k - 1],
            recv_sem=b_rsem.at[p, k - 1],
            device_id=ad_peer(k),
            device_id_type=MESH,
        )

    def s1_copy(p, j):
        return pltpu.make_async_remote_copy(
            src_ref=send1.at[p, j],
            dst_ref=recv1.at[p, j],
            send_sem=s1_ssem.at[p, j],
            recv_sem=s1_rsem.at[p, j],
            device_id={"tp": me_x * 2 + 1 - core},
            device_id_type=MESH,
        )

    def s2_copy(p, j, k):
        return pltpu.make_async_remote_copy(
            src_ref=send2.at[p, j, k - 1],
            dst_ref=recv2.at[p, j, k - 1],
            send_sem=s2_ssem.at[p, j, k - 1],
            recv_sem=s2_rsem.at[p, j, k - 1],
            device_id={"tp": lax.rem(me_x + k, n_x) * 2 + core},
            device_id_type=MESH,
        )

    for p in range(PHASES):
        own_copy(p).start()
    dn_copy.start()

    barrier = pltpu.get_barrier_semaphore()
    for k in range(1, n_ad):
        pl.semaphore_signal(barrier, inc=1, device_id=ad_peer(k), device_id_type=MESH)
    for k in range(1, n_tp):
        pl.semaphore_signal(barrier, inc=1, device_id=tp_peer(k), device_id_type=MESH)
    for j in range(CHUNKS):
        w_copy(j).start()
    up_copy.start()

    own_ids = ids[...]
    own_slots = jnp.zeros(own_ids.shape, F32)
    for a in range(table.shape[0]):
        own_slots = jnp.where(own_ids == a, table[a].astype(F32), own_slots)
    own_slots = jnp.broadcast_to(own_slots, (8, rows_dev)).astype(BF16)
    source = lax.broadcasted_iota(jnp.int32, (rows_dev, rows), 0)
    lane = lax.broadcasted_iota(jnp.int32, (rows_dev, rows), 1)
    for p in range(PHASES):
        inside = jnp.logical_and(source >= p * hp, source < (p + 1) * hp)
        place = jnp.logical_and(inside, lane == me_ad * hp + source - p * hp)
        onehot = jnp.where(place, 1.0, 0.0).astype(BF16)
        meta_own[p] = jnp.dot(own_slots, onehot, preferred_element_type=F32)

    pl.semaphore_wait(barrier, n_ad + n_tp - 2)
    for k in range(1, n_ad):
        m_copy(k).start()
    for k in range(1, n_ad):
        x_send(0, k).start()
    for k in range(1, n_ad):
        m_copy(k).wait_recv()
    for p in range(PHASES):
        total = meta_own[p]
        for k in range(1, n_ad):
            total += meta_in[k - 1, p]
        slots[p] = total
        slot_row = total[0:1]
        scale_row = jnp.zeros((1, rows), F32)
        for s in range(n_slots):
            scale_row = jnp.where(slot_row == float(s), scales[s], scale_row)
        scale_cols[p] = jnp.broadcast_to(scale_row, (128, rows)).T
    dn_copy.wait()

    def base(p, first, last):
        @pl.loop(first, last)
        def _(j):
            if p == 0:
                w_copy(j).wait()

            @pl.loop(0, cw // tile)
            def _(i):
                at = pl.ds(pl.multiple_of(j * cw + i * tile, tile), tile)
                acc[:, at] = jnp.dot(x_all[p], w[:, at], preferred_element_type=F32)

    def forward(p, j):
        s1_copy(p, j).wait_recv()
        for k in range(1, n_x):
            at = lax.rem(me_x + k, n_x)
            both = keep[p, j, at].astype(F32) + recv1[p, j, at].astype(F32)
            send2[p, j, k - 1] = both.astype(BF16)
            s2_copy(p, j, k).start()

    def finish(p):
        @pl.loop(0, CHUNKS)
        def _(j):
            total = keep[p, j, me_x].astype(F32) + recv1[p, j, me_x].astype(F32)
            for k in range(1, n_x):
                s2_copy(p, j, k).wait_recv()
                total += recv2[p, j, k - 1].astype(F32)
            total = total.astype(BF16)
            for b in range(blocks):
                out[pl.ds(b * rows_dev + p * hp, hp), cols(j)] = total[b * hp : (b + 1) * hp]

    for p in range(PHASES):
        own_copy(p).wait()
        for k in range(1, n_ad):
            x_recv(p, k).wait_recv()
        if p + 1 < PHASES:
            for k in range(1, n_ad):
                x_send(p, k).wait_send()
            for k in range(1, n_ad):
                x_send(p + 1, k).start()

        slot_row = slots[p][0:1]
        partial = lax.dot_general(
            dn[...], x_all[p], (((1,), (1,)), ((), ())), preferred_element_type=F32
        )
        mine = jnp.zeros((rank, rows), F32)
        for h in range(owned):
            here = (me_ad * owned + h).astype(F32)
            mine = jnp.where(slot_row == here, partial[h * rank : (h + 1) * rank], mine)
        for t in range(n_tp):
            a_send[p, t] = mine[t * rank_part : (t + 1) * rank_part]
        for k in range(1, n_tp):
            a_copy(p, k).start()

        base(p, 0, EARLY)

        total = a_send[p, me_tp]
        for k in range(1, n_tp):
            a_copy(p, k).wait_recv()
            total += a_recv[p, k - 1]
        b_send[p] = total.astype(BF16).astype(F32)
        for k in range(1, n_ad):
            b_copy(p, k).start()

        base(p, EARLY, CHUNKS)

        shrunk = b_send[p]
        for k in range(1, n_ad):
            b_copy(p, k).wait_recv()
            shrunk += b_recv[p, k - 1]
        for s in range(n_slots):
            spread[pl.ds(s * rank_part, rank_part)] = jnp.where(slot_row == float(s), shrunk, 0.0)
        expand[...] = spread[...].T.astype(BF16)
        if p == 0:
            up_copy.wait()

        @pl.loop(0, CHUNKS)
        def _(j):
            delta = jnp.dot(expand[...], upv[:, cols(j)], preferred_element_type=F32)
            term = acc[:, cols(j)] + scale_cols[p][:, 0:1] * delta
            term = term.astype(BF16)
            for x in range(n_x):
                even = term[2 * x * per_dest : (2 * x + 1) * per_dest]
                odd = term[(2 * x + 1) * per_dest : (2 * x + 2) * per_dest]
                send1[p, j, x] = jnp.where(core == 0, odd, even)
                keep[p, j, x] = jnp.where(core == 0, even, odd)
            s1_copy(p, j).start()

            @pl.when(j > 0)
            def _():
                forward(p, j - 1)

        forward(p, CHUNKS - 1)

    for p in range(PHASES):
        finish(p)

    for k in range(1, n_ad):
        m_copy(k).wait_send()
        x_send(PHASES - 1, k).wait_send()
    for p in range(PHASES):
        for k in range(1, n_tp):
            a_copy(p, k).wait_send()
        for k in range(1, n_ad):
            b_copy(p, k).wait_send()

        @pl.loop(0, CHUNKS)
        def _(j):
            s1_copy(p, j).wait_send()
            for k in range(1, n_x):
                s2_copy(p, j, k).wait_send()


def per_device(
    tokens,
    row_adapter_index,
    adapter_slot_table,
    gate_matrix,
    down_weight_slots,
    up_weight_slots,
    slot_scale_table,
):
    n_ad = lax.axis_size("ad")
    n_tp = lax.axis_size("tp")
    rows_dev, depth = tokens.shape
    width = gate_matrix.shape[1]
    owned, rank, _ = down_weight_slots.shape
    n_slots, rank_part, _ = up_weight_slots.shape
    hp = rows_dev // PHASES
    rows = n_ad * hp
    n_x = n_tp // 2
    per_dest = rows // n_tp
    cw = width // CHUNKS
    out_rows = rows_dev * n_ad // n_tp
    vmem = pl.BlockSpec(memory_space=pltpu.VMEM)
    smem = pl.BlockSpec(memory_space=pltpu.SMEM)
    hbm = pl.BlockSpec(memory_space=pl.ANY)
    dma = pltpu.SemaphoreType.DMA
    return pl.pallas_call(
        functools.partial(kernel, n_ad, n_tp),
        out_shape=jax.ShapeDtypeStruct((out_rows, width), BF16),
        in_specs=[hbm, vmem, smem, smem, hbm, hbm, hbm],
        out_specs=vmem,
        scratch_shapes=[
            pltpu.VMEM((PHASES, rows, depth), BF16),
            pltpu.VMEM((depth, width), BF16),
            pltpu.VMEM((owned * rank, depth), BF16),
            pltpu.VMEM((n_slots * rank_part, width), BF16),
            pltpu.VMEM((rows, width), F32),
            pltpu.VMEM((PHASES, 8, rows), F32),
            pltpu.VMEM((n_ad - 1, PHASES, 8, rows), F32),
            pltpu.VMEM((PHASES, 8, rows), F32),
            pltpu.VMEM((PHASES, rows, 128), F32),
            pltpu.VMEM((PHASES, n_tp, rank_part, rows), F32),
            pltpu.VMEM((PHASES, n_tp - 1, rank_part, rows), F32),
            pltpu.VMEM((PHASES, rank_part, rows), F32),
            pltpu.VMEM((PHASES, n_ad - 1, rank_part, rows), F32),
            pltpu.VMEM((n_slots * rank_part, rows), F32),
            pltpu.VMEM((rows, n_slots * rank_part), BF16),
            pltpu.VMEM((PHASES, CHUNKS, n_x, per_dest, cw), BF16),
            pltpu.VMEM((PHASES, CHUNKS, n_x, per_dest, cw), BF16),
            pltpu.VMEM((PHASES, CHUNKS, n_x, per_dest, cw), BF16),
            pltpu.VMEM((PHASES, CHUNKS, n_x - 1, per_dest, cw), BF16),
            pltpu.VMEM((PHASES, CHUNKS, n_x - 1, per_dest, cw), BF16),
            dma((CHUNKS,)),
            dma((2 + PHASES,)),
            dma((PHASES, n_ad - 1)),
            dma((PHASES, n_ad - 1)),
            dma((n_ad - 1,)),
            dma((n_ad - 1,)),
            dma((PHASES, n_tp - 1)),
            dma((PHASES, n_tp - 1)),
            dma((PHASES, n_ad - 1)),
            dma((PHASES, n_ad - 1)),
            dma((PHASES, CHUNKS)),
            dma((PHASES, CHUNKS)),
            dma((PHASES, CHUNKS, n_x - 1)),
            dma((PHASES, CHUNKS, n_x - 1)),
        ],
        compiler_params=pltpu.CompilerParams(
            collective_id=0, has_side_effects=True, vmem_limit_bytes=60 * 1024 * 1024
        ),
    )(
        tokens,
        row_adapter_index.reshape(1, rows_dev),
        adapter_slot_table,
        slot_scale_table,
        gate_matrix,
        down_weight_slots.reshape(owned * rank, depth),
        up_weight_slots.reshape(n_slots * rank_part, width),
    )


def solution(mesh):
    in_specs = (
        P(("grp", "ad"), "tp"),
        P(("grp", "ad")),
        P("grp"),
        P("tp", "ad"),
        P("ad", None, "tp"),
        P(None, "tp", "ad"),
        P(),
    )
    out_specs = P(("grp", "tp"), "ad")
    return jax.shard_map(
        per_device, mesh=mesh, in_specs=in_specs, out_specs=out_specs, check_vma=False
    )
```

```python
import functools

import jax
import jax.numpy as jnp
from jax import lax
from jax.experimental import pallas as pl
from jax.experimental.pallas import tpu as pltpu
from jax.sharding import PartitionSpec as P

PHASES = 2
CHUNKS = 7
MESH = pl.DeviceIdType.MESH
F32 = jnp.float32
BF16 = jnp.bfloat16


def kernel(
    n_ad,
    n_tp,
    tokens,
    ids,
    table,
    scales,
    gate,
    down,
    up,
    out,
    x_all,
    w,
    dn,
    upv,
    acc,
    meta_own,
    meta_in,
    slots,
    scale_cols,
    a_send,
    a_recv,
    b_send,
    b_recv,
    spread,
    expand,
    send1,
    recv1,
    keep,
    send2,
    recv2,
    w_sem,
    local_sem,
    x_ssem,
    x_rsem,
    m_ssem,
    m_rsem,
    a_ssem,
    a_rsem,
    b_ssem,
    b_rsem,
    s1_ssem,
    s1_rsem,
    s2_ssem,
    s2_rsem,
):
    me_ad = lax.axis_index("ad")
    me_tp = lax.axis_index("tp")
    core = lax.rem(me_tp, 2)
    me_x = me_tp // 2
    n_x = n_tp // 2
    rows_dev = tokens.shape[0]
    hp = rows_dev // PHASES
    rows = n_ad * hp
    cw = gate.shape[1] // CHUNKS
    tile = 512 if cw % 512 == 0 else cw
    rank_part = a_recv.shape[2]
    rank = rank_part * n_tp
    owned = down.shape[0] // rank
    n_slots = scales.shape[0]
    per_dest = rows // n_tp
    blocks = n_ad // n_tp

    def cols(j):
        return pl.ds(pl.multiple_of(j * cw, cw), cw)

    def ad_peer(k):
        return {"ad": lax.rem(me_ad + k, n_ad)}

    def tp_peer(k):
        return {"tp": lax.rem(me_tp + k, n_tp)}

    def w_copy(j):
        return pltpu.make_async_copy(gate.at[:, cols(j)], w.at[:, cols(j)], w_sem.at[j])

    dn_copy = pltpu.make_async_copy(down, dn, local_sem.at[0])
    up_copy = pltpu.make_async_copy(up, upv, local_sem.at[1])

    def own_rows(p):
        return x_all.at[p, pl.ds(pl.multiple_of(me_ad * hp, hp), hp)]

    def own_copy(p):
        return pltpu.make_async_copy(
            tokens.at[pl.ds(p * hp, hp)], own_rows(p), local_sem.at[2 + p]
        )

    def hop(p, s, way, block):
        block = lax.rem(block + n_ad, n_ad)
        at = pl.ds(pl.multiple_of(block * hp, hp), hp)
        return pltpu.make_async_remote_copy(
            src_ref=tokens.at[pl.ds(p * hp, hp)] if s == 1 else x_all.at[p, at],
            dst_ref=x_all.at[p, at],
            send_sem=x_ssem.at[p, (1 - way) // 2, s - 1],
            recv_sem=x_rsem.at[p, (1 - way) // 2, s - 1],
            device_id={"ad": lax.rem(me_ad + way + n_ad, n_ad)},
            device_id_type=MESH,
        )

    def sends(s, way):
        if way > 0:
            return jnp.logical_and(me_ad < n_ad - 1, me_ad >= s - 1)
        return jnp.logical_and(me_ad > 0, me_ad <= n_ad - s)

    def hop_start(p, s):
        for way in (1, -1):

            @pl.when(sends(s, way))
            def _():
                hop(p, s, way, me_ad - way * (s - 1)).start()

    def hop_sent(p, s):
        for way in (1, -1):

            @pl.when(sends(s, way))
            def _():
                hop(p, s, way, me_ad - way * (s - 1)).wait_send()

    def hop_recv(p, s):
        for way in (1, -1):

            @pl.when(me_ad >= s if way > 0 else me_ad <= n_ad - 1 - s)
            def _():
                hop(p, s, way, me_ad - way * s).wait_recv()

    def m_copy(k):
        return pltpu.make_async_remote_copy(
            src_ref=meta_own,
            dst_ref=meta_in.at[k - 1],
            send_sem=m_ssem.at[k - 1],
            recv_sem=m_rsem.at[k - 1],
            device_id=ad_peer(k),
            device_id_type=MESH,
        )

    def a_copy(p, k):
        return pltpu.make_async_remote_copy(
            src_ref=a_send.at[p, lax.rem(me_tp + k, n_tp)],
            dst_ref=a_recv.at[p, k - 1],
            send_sem=a_ssem.at[p, k - 1],
            recv_sem=a_rsem.at[p, k - 1],
            device_id=tp_peer(k),
            device_id_type=MESH,
        )

    def b_copy(p, k):
        return pltpu.make_async_remote_copy(
            src_ref=b_send.at[p],
            dst_ref=b_recv.at[p, k - 1],
            send_sem=b_ssem.at[p, k - 1],
            recv_sem=b_rsem.at[p, k - 1],
            device_id=ad_peer(k),
            device_id_type=MESH,
        )

    def s1_copy(p, j, k):
        at = lax.rem(me_x + k, n_x)
        return pltpu.make_async_remote_copy(
            src_ref=send1.at[p, j, at],
            dst_ref=recv1.at[p, j, at],
            send_sem=s1_ssem.at[p, j, k],
            recv_sem=s1_rsem.at[p, j, k],
            device_id={"tp": me_x * 2 + 1 - core},
            device_id_type=MESH,
        )

    def s2_copy(p, j, k):
        return pltpu.make_async_remote_copy(
            src_ref=send2.at[p, j, k - 1],
            dst_ref=recv2.at[p, j, k - 1],
            send_sem=s2_ssem.at[p, j, k - 1],
            recv_sem=s2_rsem.at[p, j, k - 1],
            device_id={"tp": lax.rem(me_x + k, n_x) * 2 + core},
            device_id_type=MESH,
        )

    for p in range(PHASES):
        own_copy(p).start()
    dn_copy.start()

    barrier = pltpu.get_barrier_semaphore()
    for k in range(1, n_ad):
        pl.semaphore_signal(barrier, inc=1, device_id=ad_peer(k), device_id_type=MESH)
    for k in range(1, n_tp):
        pl.semaphore_signal(barrier, inc=1, device_id=tp_peer(k), device_id_type=MESH)
    for j in range(CHUNKS):
        w_copy(j).start()
    up_copy.start()

    own_ids = ids[...]
    own_slots = jnp.zeros(own_ids.shape, F32)
    for a in range(table.shape[0]):
        own_slots = jnp.where(own_ids == a, table[a].astype(F32), own_slots)
    own_slots = jnp.broadcast_to(own_slots, (8, rows_dev)).astype(BF16)
    source = lax.broadcasted_iota(jnp.int32, (rows_dev, rows), 0)
    lane = lax.broadcasted_iota(jnp.int32, (rows_dev, rows), 1)
    for p in range(PHASES):
        inside = jnp.logical_and(source >= p * hp, source < (p + 1) * hp)
        place = jnp.logical_and(inside, lane == me_ad * hp + source - p * hp)
        onehot = jnp.where(place, 1.0, 0.0).astype(BF16)
        meta_own[p] = jnp.dot(own_slots, onehot, preferred_element_type=F32)

    pl.semaphore_wait(barrier, n_ad + n_tp - 2)
    for k in range(1, n_ad):
        m_copy(k).start()
    hop_start(0, 1)
    for k in range(1, n_ad):
        m_copy(k).wait_recv()
    for p in range(PHASES):
        total = meta_own[p]
        for k in range(1, n_ad):
            total += meta_in[k - 1, p]
        slots[p] = total
        slot_row = total[0:1]
        scale_row = jnp.zeros((1, rows), F32)
        for s in range(n_slots):
            scale_row = jnp.where(slot_row == float(s), scales[s], scale_row)
        scale_cols[p] = jnp.broadcast_to(scale_row, (128, rows)).T
    dn_copy.wait()

    def base(p, j):
        if p == 0:
            w_copy(j).wait()

        @pl.loop(0, cw // tile)
        def _(i):
            at = pl.ds(pl.multiple_of(j * cw + i * tile, tile), tile)
            acc[p, :, at] = jnp.dot(x_all[p], w[:, at], preferred_element_type=F32)

    def forward(p, j):
        for k in range(1, n_x):
            s1_copy(p, j, k).wait_recv()
            at = lax.rem(me_x + k, n_x)
            both = keep[p, j, at].astype(F32) + recv1[p, j, at].astype(F32)
            send2[p, j, k - 1] = both.astype(BF16)
            s2_copy(p, j, k).start()

    def finish(p, j):
        s1_copy(p, j, 0).wait_recv()
        total = keep[p, j, me_x].astype(F32) + recv1[p, j, me_x].astype(F32)
        for k in range(1, n_x):
            s2_copy(p, j, k).wait_recv()
            total += recv2[p, j, k - 1].astype(F32)
        total = total.astype(BF16)
        for b in range(blocks):
            out[pl.ds(b * rows_dev + p * hp, hp), cols(j)] = total[b * hp : (b + 1) * hp]

    def shrink(p):
        own_copy(p).wait()
        slot_row = slots[p][0:1]
        partial = lax.dot_general(
            dn[...], x_all[p], (((1,), (1,)), ((), ())), preferred_element_type=F32
        )
        mine = jnp.zeros((rank, rows), F32)
        for h in range(owned):
            here = (me_ad * owned + h).astype(F32)
            mine = jnp.where(slot_row == here, partial[h * rank : (h + 1) * rank], mine)
        for t in range(n_tp):
            a_send[p, t] = mine[t * rank_part : (t + 1) * rank_part]
        for k in range(1, n_tp):
            a_copy(p, k).start()

    def share(p):
        total = a_send[p, me_tp]
        for k in range(1, n_tp):
            a_copy(p, k).wait_recv()
            total += a_recv[p, k - 1]
        b_send[p] = total.astype(BF16).astype(F32)
        for k in range(1, n_ad):
            b_copy(p, k).start()

    def widen(p):
        slot_row = slots[p][0:1]
        shrunk = b_send[p]
        for k in range(1, n_ad):
            b_copy(p, k).wait_recv()
            shrunk += b_recv[p, k - 1]
        for s in range(n_slots):
            spread[pl.ds(s * rank_part, rank_part)] = jnp.where(slot_row == float(s), shrunk, 0.0)
        expand[p] = spread[...].T.astype(BF16)

    def term(p, j):
        delta = jnp.dot(expand[p], upv[:, cols(j)], preferred_element_type=F32)
        value = acc[p, :, cols(j)] + scale_cols[p][:, 0:1] * delta
        value = value.astype(BF16)
        for x in range(n_x):
            even = value[2 * x * per_dest : (2 * x + 1) * per_dest]
            odd = value[(2 * x + 1) * per_dest : (2 * x + 2) * per_dest]
            send1[p, j, x] = jnp.where(core == 0, odd, even)
            keep[p, j, x] = jnp.where(core == 0, even, odd)
        for k in list(range(1, n_x)) + [0]:
            s1_copy(p, j, k).start()

    for s in range(1, n_ad):
        if s > 1:
            hop_start(0, s)
        hop_recv(0, s)
    hop_start(1, 1)
    shrink(0)
    pl.loop(0, 2)(lambda j: base(0, j))
    share(0)
    half = n_ad // 2
    for s in range(1, half):
        hop_recv(1, s)
        hop_start(1, s + 1)
    pl.loop(2, 5)(lambda j: base(0, j))
    for s in range(half, n_ad - 1):
        hop_recv(1, s)
        hop_start(1, s + 1)
    up_copy.wait()
    widen(0)

    @pl.loop(0, 2)
    def _(j):
        term(0, j)
        base(0, j + 5)
        forward(0, j)

    term(0, 2)
    hop_recv(1, n_ad - 1)
    shrink(1)
    forward(0, 2)

    @pl.loop(3, 7)
    def _(j):
        term(0, j)
        base(1, j - 3)

        @pl.when(j == 4)
        def _():
            share(1)

        forward(0, j)

    widen(1)

    @pl.loop(0, 3)
    def _(j):
        term(1, j)
        base(1, j + 4)
        forward(1, j)
        finish(0, j)

    @pl.loop(3, 7)
    def _(j):
        term(1, j)
        finish(0, j)
        forward(1, j)

    pl.loop(0, CHUNKS)(lambda j: finish(1, j))

    for k in range(1, n_ad):
        m_copy(k).wait_send()
    for p in range(PHASES):
        for s in range(1, n_ad):
            hop_sent(p, s)
        for k in range(1, n_tp):
            a_copy(p, k).wait_send()
        for k in range(1, n_ad):
            b_copy(p, k).wait_send()

        @pl.loop(0, CHUNKS)
        def _(j):
            for k in range(n_x):
                s1_copy(p, j, k).wait_send()
            for k in range(1, n_x):
                s2_copy(p, j, k).wait_send()


def per_device(
    tokens,
    row_adapter_index,
    adapter_slot_table,
    gate_matrix,
    down_weight_slots,
    up_weight_slots,
    slot_scale_table,
):
    n_ad = lax.axis_size("ad")
    n_tp = lax.axis_size("tp")
    rows_dev, depth = tokens.shape
    width = gate_matrix.shape[1]
    owned, rank, _ = down_weight_slots.shape
    n_slots, rank_part, _ = up_weight_slots.shape
    hp = rows_dev // PHASES
    rows = n_ad * hp
    n_x = n_tp // 2
    per_dest = rows // n_tp
    cw = width // CHUNKS
    out_rows = rows_dev * n_ad // n_tp
    vmem = pl.BlockSpec(memory_space=pltpu.VMEM)
    smem = pl.BlockSpec(memory_space=pltpu.SMEM)
    hbm = pl.BlockSpec(memory_space=pl.ANY)
    dma = pltpu.SemaphoreType.DMA
    return pl.pallas_call(
        functools.partial(kernel, n_ad, n_tp),
        out_shape=jax.ShapeDtypeStruct((out_rows, width), BF16),
        in_specs=[hbm, vmem, smem, smem, hbm, hbm, hbm],
        out_specs=vmem,
        scratch_shapes=[
            pltpu.VMEM((PHASES, rows, depth), BF16),
            pltpu.VMEM((depth, width), BF16),
            pltpu.VMEM((owned * rank, depth), BF16),
            pltpu.VMEM((n_slots * rank_part, width), BF16),
            pltpu.VMEM((PHASES, rows, width), F32),
            pltpu.VMEM((PHASES, 8, rows), F32),
            pltpu.VMEM((n_ad - 1, PHASES, 8, rows), F32),
            pltpu.VMEM((PHASES, 8, rows), F32),
            pltpu.VMEM((PHASES, rows, 128), F32),
            pltpu.VMEM((PHASES, n_tp, rank_part, rows), F32),
            pltpu.VMEM((PHASES, n_tp - 1, rank_part, rows), F32),
            pltpu.VMEM((PHASES, rank_part, rows), F32),
            pltpu.VMEM((PHASES, n_ad - 1, rank_part, rows), F32),
            pltpu.VMEM((n_slots * rank_part, rows), F32),
            pltpu.VMEM((PHASES, rows, n_slots * rank_part), BF16),
            pltpu.VMEM((PHASES, CHUNKS, n_x, per_dest, cw), BF16),
            pltpu.VMEM((PHASES, CHUNKS, n_x, per_dest, cw), BF16),
            pltpu.VMEM((PHASES, CHUNKS, n_x, per_dest, cw), BF16),
            pltpu.VMEM((PHASES, CHUNKS, n_x - 1, per_dest, cw), BF16),
            pltpu.VMEM((PHASES, CHUNKS, n_x - 1, per_dest, cw), BF16),
            dma((CHUNKS,)),
            dma((2 + PHASES,)),
            dma((PHASES, 2, n_ad - 1)),
            dma((PHASES, 2, n_ad - 1)),
            dma((n_ad - 1,)),
            dma((n_ad - 1,)),
            dma((PHASES, n_tp - 1)),
            dma((PHASES, n_tp - 1)),
            dma((PHASES, n_ad - 1)),
            dma((PHASES, n_ad - 1)),
            dma((PHASES, CHUNKS, n_x)),
            dma((PHASES, CHUNKS, n_x)),
            dma((PHASES, CHUNKS, n_x - 1)),
            dma((PHASES, CHUNKS, n_x - 1)),
        ],
        compiler_params=pltpu.CompilerParams(
            collective_id=0, has_side_effects=True, vmem_limit_bytes=60 * 1024 * 1024
        ),
    )(
        tokens,
        row_adapter_index.reshape(1, rows_dev),
        adapter_slot_table,
        slot_scale_table,
        gate_matrix,
        down_weight_slots.reshape(owned * rank, depth),
        up_weight_slots.reshape(n_slots * rank_part, width),
    )


def solution(mesh):
    in_specs = (
        P(("grp", "ad"), "tp"),
        P(("grp", "ad")),
        P("grp"),
        P("tp", "ad"),
        P("ad", None, "tp"),
        P(None, "tp", "ad"),
        P(),
    )
    out_specs = P(("grp", "tp"), "ad")
    return jax.shard_map(
        per_device, mesh=mesh, in_specs=in_specs, out_specs=out_specs, check_vma=False
    )
```

```python
import functools

import jax
import jax.numpy as jnp
from jax import lax
from jax.experimental import pallas as pl
from jax.experimental.pallas import tpu as pltpu
from jax.sharding import PartitionSpec as P

PHASES = 2
CHUNKS = 7
MESH = pl.DeviceIdType.MESH
F32 = jnp.float32
BF16 = jnp.bfloat16


def kernel(
    n_ad,
    n_tp,
    tokens,
    ids,
    table,
    scales,
    gate,
    down,
    up,
    out,
    x_all,
    w,
    dn,
    upv,
    acc,
    meta_own,
    meta_in,
    slots,
    scale_cols,
    a_send,
    a_recv,
    b_send,
    b_recv,
    spread,
    expand,
    send1,
    recv1,
    keep,
    send2,
    recv2,
    w_sem,
    local_sem,
    x_ssem,
    x_rsem,
    m_ssem,
    m_rsem,
    a_ssem,
    a_rsem,
    b_ssem,
    b_rsem,
    s1_ssem,
    s1_rsem,
    s2_ssem,
    s2_rsem,
):
    me_ad = lax.axis_index("ad")
    me_tp = lax.axis_index("tp")
    core = lax.rem(me_tp, 2)
    me_x = me_tp // 2
    n_x = n_tp // 2
    rows_dev = tokens.shape[0]
    hp = rows_dev // PHASES
    rows = n_ad * hp
    cw = gate.shape[1] // CHUNKS
    tile = 512 if cw % 512 == 0 else cw
    rank_part = a_recv.shape[2]
    rank = rank_part * n_tp
    owned = down.shape[0] // rank
    n_slots = scales.shape[0]
    per_dest = rows // n_tp
    blocks = n_ad // n_tp

    def cols(j):
        return pl.ds(pl.multiple_of(j * cw, cw), cw)

    def ad_peer(k):
        return {"ad": lax.rem(me_ad + k, n_ad)}

    def tp_peer(k):
        return {"tp": lax.rem(me_tp + k, n_tp)}

    def w_copy(j):
        return pltpu.make_async_copy(gate.at[:, cols(j)], w.at[:, cols(j)], w_sem.at[j])

    dn_copy = pltpu.make_async_copy(down, dn, local_sem.at[0])
    up_copy = pltpu.make_async_copy(up, upv, local_sem.at[1])

    def own_rows(p):
        return x_all.at[p, pl.ds(pl.multiple_of(me_ad * hp, hp), hp)]

    def own_copy(p):
        return pltpu.make_async_copy(
            tokens.at[pl.ds(p * hp, hp)], own_rows(p), local_sem.at[2 + p]
        )

    def hop(p, s, way, block):
        block = lax.rem(block + n_ad, n_ad)
        at = pl.ds(pl.multiple_of(block * hp, hp), hp)
        return pltpu.make_async_remote_copy(
            src_ref=tokens.at[pl.ds(p * hp, hp)] if s == 1 else x_all.at[p, at],
            dst_ref=x_all.at[p, at],
            send_sem=x_ssem.at[p, (1 - way) // 2, s - 1],
            recv_sem=x_rsem.at[p, (1 - way) // 2, s - 1],
            device_id={"ad": lax.rem(me_ad + way + n_ad, n_ad)},
            device_id_type=MESH,
        )

    def sends(s, way):
        if way > 0:
            return jnp.logical_and(me_ad < n_ad - 1, me_ad >= s - 1)
        return jnp.logical_and(me_ad > 0, me_ad <= n_ad - s)

    def hop_start(p, s):
        for way in (1, -1):

            @pl.when(sends(s, way))
            def _():
                hop(p, s, way, me_ad - way * (s - 1)).start()

    def hop_sent(p, s):
        for way in (1, -1):

            @pl.when(sends(s, way))
            def _():
                hop(p, s, way, me_ad - way * (s - 1)).wait_send()

    def hop_recv(p, s):
        for way in (1, -1):

            @pl.when(me_ad >= s if way > 0 else me_ad <= n_ad - 1 - s)
            def _():
                hop(p, s, way, me_ad - way * s).wait_recv()

    def m_copy(k):
        return pltpu.make_async_remote_copy(
            src_ref=meta_own,
            dst_ref=meta_in.at[k - 1],
            send_sem=m_ssem.at[k - 1],
            recv_sem=m_rsem.at[k - 1],
            device_id=ad_peer(k),
            device_id_type=MESH,
        )

    def a_copy(p, k):
        return pltpu.make_async_remote_copy(
            src_ref=a_send.at[p, lax.rem(me_tp + k, n_tp)],
            dst_ref=a_recv.at[p, k - 1],
            send_sem=a_ssem.at[p, k - 1],
            recv_sem=a_rsem.at[p, k - 1],
            device_id=tp_peer(k),
            device_id_type=MESH,
        )

    def b_copy(p, k):
        return pltpu.make_async_remote_copy(
            src_ref=b_send.at[p],
            dst_ref=b_recv.at[p, k - 1],
            send_sem=b_ssem.at[p, k - 1],
            recv_sem=b_rsem.at[p, k - 1],
            device_id=ad_peer(k),
            device_id_type=MESH,
        )

    def s1_copy(p, j, k):
        at = lax.rem(me_x + k, n_x)
        return pltpu.make_async_remote_copy(
            src_ref=send1.at[p, j, at],
            dst_ref=recv1.at[p, j, at],
            send_sem=s1_ssem.at[p, j, k],
            recv_sem=s1_rsem.at[p, j, k],
            device_id={"tp": me_x * 2 + 1 - core},
            device_id_type=MESH,
        )

    def s2_copy(p, j, k):
        return pltpu.make_async_remote_copy(
            src_ref=send2.at[p, j, k - 1],
            dst_ref=recv2.at[p, j, k - 1],
            send_sem=s2_ssem.at[p, j, k - 1],
            recv_sem=s2_rsem.at[p, j, k - 1],
            device_id={"tp": lax.rem(me_x + k, n_x) * 2 + core},
            device_id_type=MESH,
        )

    for p in range(PHASES):
        own_copy(p).start()
    dn_copy.start()

    barrier = pltpu.get_barrier_semaphore()
    for k in range(1, n_ad):
        pl.semaphore_signal(barrier, inc=1, device_id=ad_peer(k), device_id_type=MESH)
    for k in range(1, n_tp):
        pl.semaphore_signal(barrier, inc=1, device_id=tp_peer(k), device_id_type=MESH)
    for j in range(CHUNKS):
        w_copy(j).start()
    up_copy.start()

    own_ids = ids[...]
    own_slots = jnp.zeros(own_ids.shape, F32)
    for a in range(table.shape[0]):
        own_slots = jnp.where(own_ids == a, table[a].astype(F32), own_slots)
    own_slots = jnp.broadcast_to(own_slots, (8, rows_dev)).astype(BF16)
    source = lax.broadcasted_iota(jnp.int32, (rows_dev, rows), 0)
    lane = lax.broadcasted_iota(jnp.int32, (rows_dev, rows), 1)
    for p in range(PHASES):
        inside = jnp.logical_and(source >= p * hp, source < (p + 1) * hp)
        place = jnp.logical_and(inside, lane == me_ad * hp + source - p * hp)
        onehot = jnp.where(place, 1.0, 0.0).astype(BF16)
        meta_own[p] = jnp.dot(own_slots, onehot, preferred_element_type=F32)

    pl.semaphore_wait(barrier, n_ad + n_tp - 2)
    for k in range(1, n_ad):
        m_copy(k).start()
    hop_start(0, 1)
    for k in range(1, n_ad):
        m_copy(k).wait_recv()
    for p in range(PHASES):
        total = meta_own[p]
        for k in range(1, n_ad):
            total += meta_in[k - 1, p]
        slots[p] = total
        slot_row = total[0:1]
        scale_row = jnp.zeros((1, rows), F32)
        for s in range(n_slots):
            scale_row = jnp.where(slot_row == float(s), scales[s], scale_row)
        scale_cols[p] = jnp.broadcast_to(scale_row, (128, rows)).T
    dn_copy.wait()

    def base(p, j):
        if p == 0:
            w_copy(j).wait()

        @pl.loop(0, cw // tile)
        def _(i):
            at = pl.ds(pl.multiple_of(j * cw + i * tile, tile), tile)
            acc[p, :, at] = jnp.dot(x_all[p], w[:, at], preferred_element_type=F32)

    def forward(p, j):
        for k in range(1, n_x):
            s1_copy(p, j, k).wait_recv()
            at = lax.rem(me_x + k, n_x)
            both = keep[p, j, at].astype(F32) + recv1[p, j, at].astype(F32)
            send2[p, j, k - 1] = both.astype(BF16)
            s2_copy(p, j, k).start()

    def finish(p, j):
        s1_copy(p, j, 0).wait_recv()
        total = keep[p, j, me_x].astype(F32) + recv1[p, j, me_x].astype(F32)
        for k in range(1, n_x):
            s2_copy(p, j, k).wait_recv()
            total += recv2[p, j, k - 1].astype(F32)
        total = total.astype(BF16)
        for b in range(blocks):
            out[pl.ds(b * rows_dev + p * hp, hp), cols(j)] = total[b * hp : (b + 1) * hp]

    def shrink(p):
        own_copy(p).wait()
        slot_row = slots[p][0:1]
        partial = lax.dot_general(
            dn[...], x_all[p], (((1,), (1,)), ((), ())), preferred_element_type=F32
        )
        mine = jnp.zeros((rank, rows), F32)
        for h in range(owned):
            here = (me_ad * owned + h).astype(F32)
            mine = jnp.where(slot_row == here, partial[h * rank : (h + 1) * rank], mine)
        for t in range(n_tp):
            a_send[p, t] = mine[t * rank_part : (t + 1) * rank_part]
        for k in range(1, n_tp):
            a_copy(p, k).start()

    def share(p):
        total = a_send[p, me_tp]
        for k in range(1, n_tp):
            a_copy(p, k).wait_recv()
            total += a_recv[p, k - 1]
        b_send[p] = total.astype(BF16).astype(F32)
        for k in range(1, n_ad):
            b_copy(p, k).start()

    def widen(p):
        slot_row = slots[p][0:1]
        shrunk = b_send[p]
        for k in range(1, n_ad):
            b_copy(p, k).wait_recv()
            shrunk += b_recv[p, k - 1]
        for s in range(n_slots):
            spread[pl.ds(s * rank_part, rank_part)] = jnp.where(slot_row == float(s), shrunk, 0.0)
        expand[p] = spread[...].T.astype(BF16)

    def term(p, j):
        delta = jnp.dot(expand[p], upv[:, cols(j)], preferred_element_type=F32)
        value = acc[p, :, cols(j)] + scale_cols[p][:, 0:1] * delta
        value = value.astype(BF16)
        for x in range(n_x):
            even = value[2 * x * per_dest : (2 * x + 1) * per_dest]
            odd = value[(2 * x + 1) * per_dest : (2 * x + 2) * per_dest]
            send1[p, j, x] = jnp.where(core == 0, odd, even)
            keep[p, j, x] = jnp.where(core == 0, even, odd)
        for k in list(range(1, n_x)) + [0]:
            s1_copy(p, j, k).start()

    for s in range(1, n_ad):
        if s > 1:
            hop_start(0, s)
        if s == n_ad - 1:
            hop_start(1, 1)
        hop_recv(0, s)
    shrink(0)
    pl.loop(0, 2)(lambda j: base(0, j))
    share(0)
    half = n_ad // 2
    for s in range(1, half):
        hop_recv(1, s)
        hop_start(1, s + 1)
    pl.loop(2, 5)(lambda j: base(0, j))
    for s in range(half, n_ad - 1):
        hop_recv(1, s)
        hop_start(1, s + 1)
    up_copy.wait()
    widen(0)

    @pl.loop(0, 2)
    def _(j):
        term(0, j)
        base(0, j + 5)
        forward(0, j)

    term(0, 2)
    hop_recv(1, n_ad - 1)
    shrink(1)
    forward(0, 2)

    @pl.loop(3, 7)
    def _(j):
        term(0, j)
        base(1, j - 3)

        @pl.when(j == 4)
        def _():
            share(1)

        forward(0, j)

    widen(1)

    @pl.loop(0, 3)
    def _(j):
        term(1, j)
        base(1, j + 4)
        forward(1, j)
        finish(0, j)

    @pl.loop(3, 7)
    def _(j):
        term(1, j)
        finish(0, j)
        forward(1, j)

    pl.loop(0, CHUNKS)(lambda j: finish(1, j))

    for k in range(1, n_ad):
        m_copy(k).wait_send()
    for p in range(PHASES):
        for s in range(1, n_ad):
            hop_sent(p, s)
        for k in range(1, n_tp):
            a_copy(p, k).wait_send()
        for k in range(1, n_ad):
            b_copy(p, k).wait_send()

        @pl.loop(0, CHUNKS)
        def _(j):
            for k in range(n_x):
                s1_copy(p, j, k).wait_send()
            for k in range(1, n_x):
                s2_copy(p, j, k).wait_send()


def per_device(
    tokens,
    row_adapter_index,
    adapter_slot_table,
    gate_matrix,
    down_weight_slots,
    up_weight_slots,
    slot_scale_table,
):
    n_ad = lax.axis_size("ad")
    n_tp = lax.axis_size("tp")
    rows_dev, depth = tokens.shape
    width = gate_matrix.shape[1]
    owned, rank, _ = down_weight_slots.shape
    n_slots, rank_part, _ = up_weight_slots.shape
    hp = rows_dev // PHASES
    rows = n_ad * hp
    n_x = n_tp // 2
    per_dest = rows // n_tp
    cw = width // CHUNKS
    out_rows = rows_dev * n_ad // n_tp
    vmem = pl.BlockSpec(memory_space=pltpu.VMEM)
    smem = pl.BlockSpec(memory_space=pltpu.SMEM)
    hbm = pl.BlockSpec(memory_space=pl.ANY)
    dma = pltpu.SemaphoreType.DMA
    return pl.pallas_call(
        functools.partial(kernel, n_ad, n_tp),
        out_shape=jax.ShapeDtypeStruct((out_rows, width), BF16),
        in_specs=[hbm, vmem, smem, smem, hbm, hbm, hbm],
        out_specs=vmem,
        scratch_shapes=[
            pltpu.VMEM((PHASES, rows, depth), BF16),
            pltpu.VMEM((depth, width), BF16),
            pltpu.VMEM((owned * rank, depth), BF16),
            pltpu.VMEM((n_slots * rank_part, width), BF16),
            pltpu.VMEM((PHASES, rows, width), F32),
            pltpu.VMEM((PHASES, 8, rows), F32),
            pltpu.VMEM((n_ad - 1, PHASES, 8, rows), F32),
            pltpu.VMEM((PHASES, 8, rows), F32),
            pltpu.VMEM((PHASES, rows, 128), F32),
            pltpu.VMEM((PHASES, n_tp, rank_part, rows), F32),
            pltpu.VMEM((PHASES, n_tp - 1, rank_part, rows), F32),
            pltpu.VMEM((PHASES, rank_part, rows), F32),
            pltpu.VMEM((PHASES, n_ad - 1, rank_part, rows), F32),
            pltpu.VMEM((n_slots * rank_part, rows), F32),
            pltpu.VMEM((PHASES, rows, n_slots * rank_part), BF16),
            pltpu.VMEM((PHASES, CHUNKS, n_x, per_dest, cw), BF16),
            pltpu.VMEM((PHASES, CHUNKS, n_x, per_dest, cw), BF16),
            pltpu.VMEM((PHASES, CHUNKS, n_x, per_dest, cw), BF16),
            pltpu.VMEM((PHASES, CHUNKS, n_x - 1, per_dest, cw), BF16),
            pltpu.VMEM((PHASES, CHUNKS, n_x - 1, per_dest, cw), BF16),
            dma((CHUNKS,)),
            dma((2 + PHASES,)),
            dma((PHASES, 2, n_ad - 1)),
            dma((PHASES, 2, n_ad - 1)),
            dma((n_ad - 1,)),
            dma((n_ad - 1,)),
            dma((PHASES, n_tp - 1)),
            dma((PHASES, n_tp - 1)),
            dma((PHASES, n_ad - 1)),
            dma((PHASES, n_ad - 1)),
            dma((PHASES, CHUNKS, n_x)),
            dma((PHASES, CHUNKS, n_x)),
            dma((PHASES, CHUNKS, n_x - 1)),
            dma((PHASES, CHUNKS, n_x - 1)),
        ],
        compiler_params=pltpu.CompilerParams(
            collective_id=0, has_side_effects=True, vmem_limit_bytes=60 * 1024 * 1024
        ),
    )(
        tokens,
        row_adapter_index.reshape(1, rows_dev),
        adapter_slot_table,
        slot_scale_table,
        gate_matrix,
        down_weight_slots.reshape(owned * rank, depth),
        up_weight_slots.reshape(n_slots * rank_part, width),
    )


def solution(mesh):
    in_specs = (
        P(("grp", "ad"), "tp"),
        P(("grp", "ad")),
        P("grp"),
        P("tp", "ad"),
        P("ad", None, "tp"),
        P(None, "tp", "ad"),
        P(),
    )
    out_specs = P(("grp", "tp"), "ad")
    return jax.shard_map(
        per_device, mesh=mesh, in_specs=in_specs, out_specs=out_specs, check_vma=False
    )
```
